32 devices in a mesh: groups: 2 (over x), chan: 16 (over z, y, core).
Axes of the slice: x: 2, y: 2, z: 4, core: 2. Of those that a mesh axis runs over, the one named last changes fastest.
Arguments:
- xz: bfloat16 [256, 2, 8192], P('groups', None, 'chan'), parts along dimension 0, may hold values from -6 to 6
- conv_state: bfloat16 [256, 3, 8192], P('groups', None, 'chan'), parts along dimension 0, may hold values from -6 to 6
- conv_weight: float32 [4, 8192], P(None, 'chan'), may hold values from -3 to 3
- conv_bias: float32 [8192], P('chan'), may hold values from -3 to 3
- ssm_state: bfloat16 [256, 16, 8192], P('groups', None, 'chan'), parts along dimension 0, may hold values from -6 to 6
- x_weight: bfloat16 [8192, 544], P('chan'), may hold values from -0.0625 to 0.0625
- dt_weight: bfloat16 [512, 8192], P(None, 'chan'), may hold values from -0.25 to 0.25
- dt_bias: float32 [8192], P('chan'), may hold values from -4 to -1
- a_log: float32 [16, 8192], P(None, 'chan'), may hold values from -1 to 2.5
- d_skip: float32 [8192], P('chan'), may hold values from 0.5 to 1.5
- out_weight: bfloat16 [8192, 4096], P('chan'), may hold values from -0.0625 to 0.0625
- residual: bfloat16 [256, 4096], P(('groups', 'chan')), parts along dimension 0, may hold values from -6 to 6
- norm_gain: float32 [4096], replicated, may hold values from 0.5 to 1.5
- expert_ids: int32 [256, 2], P(('groups', 'chan')), parts along dimension 0, may hold values from 0 to 15, all different within a row; in each aligned block of 8 rows (0 to 7, 8 to 15, ...) at most 4 rows name the same one
- route_weight: float32 [256, 2], P(('groups', 'chan')), parts along dimension 0, may hold values from 0.2 to 1
- w_gate: bfloat16 [4096, 24576], P(None, 'chan'), may hold values from -0.09375 to 0.09375
- w_up: bfloat16 [4096, 24576], P(None, 'chan'), may hold values from -0.09375 to 0.09375
- w_down: bfloat16 [24576, 4096], P('chan'), may hold values from -0.0546875 to 0.0546875
Outputs:
- result: bfloat16 [256, 4096], P(('groups', 'chan')), parts along dimension 0
- new_state: bfloat16 [256, 16, 8192], P('groups', None, 'chan'), parts along dimension 0
The draws below stay inside these ranges and needn't reach their ends.
There are 2 independent parts, one for each index of `groups`. The reference program is written for one: setup_inputs(seed, part) draws one part's arguments, and reference() takes and returns one part's arrays. A program takes and returns all parts, laid end to end along the dimension named above; an argument that names none is the same for every part. Nothing has to cross between parts.
Inputs may be any that keep to these rules, and one draw needn't show every extreme that they name: `expert_ids`: among the rows of one device, no expert is named by more than 4 rows.
All inputs are finite; a program needn't handle non-finite values.
Results may differ from the reference program's by a relative error of at most 0.006.
Values may be sent and summed in bfloat16 or wider, within the bound.
A program may use at most 128 MiB of HBM per device.

```python
import math
import jax
import jax.numpy as jnp
import numpy as np
from jax import lax

D = 4096
INNER = 8192
NSTATE = 16
RANK = 512
CONV = 4
EXPERTS = 16
HIDDEN_SIZE = 12288
FLIGHT = 2
ROW_DEV = 8
ROWS = 128
CAP = 4


def levels(stream_key, extent, shards, low, high):
    factor_of, own = 1.0, jax.random.fold_in(stream_key, 6)
    for axis_at, shards_of in shards:
        steps = jnp.exp(jax.random.uniform(jax.random.fold_in(own, axis_at), (shards_of,), jnp.float32, low / len(shards), high / len(shards)))
        factor_of = factor_of * jnp.repeat(steps, extent[axis_at] // shards_of).reshape([-1 if axis == axis_at else 1 for axis in range(len(extent))])
    return factor_of


def assign_block(rng, own, number, rows, amount, top, limit, lean):
    ranking = jax.random.permutation(rng, amount)
    heavy_load, common = portions_of(amount, rows * top, limit, lean, True), portions_of(amount, rows * top, limit, lean, False)
    places = jnp.arange(amount)

    def named(lengths, rotation):
        used = int((lengths > 0).sum())
        fixed = max(1, used // 4)
        passed = fixed + (places - fixed + rotation * (used - fixed)) % max(1, amount - fixed)
        return jnp.zeros((amount,), jnp.int32).at[ranking[jnp.where(places < fixed, places, passed)]].set(jnp.asarray(lengths, jnp.int32))

    lengths = jnp.where(number % 4 == 0, named(heavy_load, number // 4), named(common, number - number // 4 - 1))
    mixed = jax.random.permutation(jax.random.fold_in(own, 3), amount)
    giver, taker = mixed[0:amount // 2 * 2:2], mixed[1:amount // 2 * 2:2]
    room = jnp.minimum(lengths[giver] - 1, limit - lengths[taker]) // 2
    room = jnp.where((giver == ranking[0]) | (taker == ranking[0]) | (lengths[taker] == 0), 0, jnp.maximum(room, 0))
    passed = jax.random.randint(jax.random.fold_in(own, 4), (amount // 2,), 0, 1 << 20) % (room + 1)
    lengths = lengths.at[giver].add(-passed).at[taker].add(passed)
    labels = jnp.searchsorted(jnp.cumsum(lengths), jnp.arange(rows * top), side="right").astype(jnp.int32)
    grid = labels.reshape(top, rows).T
    grid = grid[jax.random.permutation(jax.random.fold_in(own, 1), rows)]
    rotation = jax.random.randint(jax.random.fold_in(own, 2), (rows, 1), 0, top)
    return jnp.take_along_axis(grid, (jnp.arange(top)[None, :] + rotation) % top, axis=1)


def portions_of(count, total, bound, skew, full):
    weights = [(1 << 20) // math.isqrt(standing ** skew) + 1 for standing in range(1, count + 1)]
    largest = bound if full else min(bound, max(-(-total // count), total * weights[0] // sum(weights)))
    least = 1 if total - largest >= count - 1 else 0
    counts, rest = [largest] + [least] * (count - 1), total - largest - least * (count - 1)
    while rest > 0:
        free = [i for i in range(1, count) if counts[i] < largest] or [i for i in range(1, count) if counts[i] < bound]
        whole, left = sum([weights[i] for i in free]), rest
        for i in free:
            addition = min(bound - counts[i], max(1, left * weights[i] // whole), rest)
            counts[i] = counts[i] + addition
            rest = rest - addition
    return np.array(counts)


def bell_draw(rng, shape, spread, most, pieces=(), held_as=jnp.bfloat16):
    values = jax.random.normal(rng, shape, jnp.float32) * spread
    if len(pieces) > 0:
        values = levels(rng, shape, pieces, -0.22, 0.18) * values
    return jnp.clip(values, min=-most, max=most).astype(held_as)


def setup_inputs(seed: int = 0, part: int = 0) -> dict:
    streams_of = jax.random.split(jax.random.key(seed), 19)
    part_keys = jax.random.split(jax.random.fold_in(streams_of[18], part), 19)
    xz = bell_draw(part_keys[0], (ROWS, 2, INNER), 1.0, 6.0, ((2, 16),))
    conv_state = bell_draw(part_keys[1], (ROWS, CONV - 1, INNER), 1.0, 6.0, ((2, 16),))
    conv_weight = bell_draw(streams_of[2], (CONV, INNER), CONV ** -0.5, 3.0, ((1, 16),), jnp.float32)
    conv_bias = bell_draw(streams_of[3], (INNER,), 0.5, 3.0, ((0, 16),), jnp.float32)
    ssm_state = bell_draw(part_keys[4], (ROWS, NSTATE, INNER), 1.0, 6.0, ((2, 16),))
    x_weight = bell_draw(streams_of[5], (INNER, RANK + 2 * NSTATE), INNER ** -0.5, 0.0625, ((0, 16),))
    dt_weight = bell_draw(streams_of[6], (RANK, INNER), RANK ** -0.5, 0.25, ((1, 16),))
    dt_bias = jnp.clip(-4.0 + 3.0 * jax.random.uniform(streams_of[7], (INNER,), jnp.float32) ** levels(streams_of[7], (INNER,), ((0, 16),), -0.2, 0.2), -4.0, -1.0)
    a_log = jnp.clip(-1.0 + 3.5 * jax.random.uniform(streams_of[8], (NSTATE, INNER), jnp.float32) ** levels(streams_of[8], (NSTATE, INNER), ((1, 16),), -0.2, 0.2), -1.0, 2.5)
    d_skip = jnp.clip(0.5 + 1.0 * jax.random.uniform(streams_of[9], (INNER,), jnp.float32) ** levels(streams_of[9], (INNER,), ((0, 16),), -0.2, 0.2), 0.5, 1.5)
    out_weight = bell_draw(streams_of[10], (INNER, D), INNER ** -0.5, 0.0625, ((0, 16),))
    residual = bell_draw(part_keys[11], (ROWS, D), 1.0, 6.0, ((0, 16),))
    norm_gain = jnp.clip(1.0 + 0.1 * jax.random.normal(streams_of[12], (D,), jnp.float32), 0.5, 1.5)
    expert_ids_keys = jax.random.split(jax.random.fold_in(part_keys[13], 1), ROWS // ROW_DEV)
    expert_ids_turns = jax.random.permutation(jax.random.fold_in(part_keys[13], 3), ROWS // ROW_DEV)
    expert_ids = jax.vmap(lambda own, number: assign_block(jax.random.fold_in(part_keys[13], 2), own, number, ROW_DEV, EXPERTS, 2, CAP, 2))(expert_ids_keys, expert_ids_turns).reshape((ROWS, 2))
    route_weight = jnp.clip(0.2 + 0.8 * jax.random.uniform(part_keys[14], (ROWS, 2), jnp.float32) ** levels(part_keys[14], (ROWS, 2), ((0, 16),), -0.2, 0.2), 0.2, 1.0)
    w_gate = bell_draw(streams_of[15], (D, FLIGHT * HIDDEN_SIZE), D ** -0.5, 0.09375, ((1, 16),))
    w_up = bell_draw(streams_of[16], (D, FLIGHT * HIDDEN_SIZE), D ** -0.5, 0.09375, ((1, 16),))
    w_down = bell_draw(streams_of[17], (FLIGHT * HIDDEN_SIZE, D), HIDDEN_SIZE ** -0.5, 0.0546875, ((0, 16),))
    return dict(xz=xz, conv_state=conv_state, conv_weight=conv_weight, conv_bias=conv_bias, ssm_state=ssm_state, x_weight=x_weight, dt_weight=dt_weight, dt_bias=dt_bias, a_log=a_log, d_skip=d_skip, out_weight=out_weight, residual=residual, norm_gain=norm_gain, expert_ids=expert_ids, route_weight=route_weight, w_gate=w_gate, w_up=w_up, w_down=w_down)


def reference(xz, conv_state, conv_weight, conv_bias, ssm_state, x_weight, dt_weight, dt_bias, a_log, d_skip, out_weight, residual, norm_gain, expert_ids, route_weight, w_gate, w_up, w_down):
    x_new = xz[:, 0, :].astype(jnp.float32)
    gate_z = xz[:, 1, :].astype(jnp.float32)
    window = jnp.concatenate([conv_state.astype(jnp.float32), x_new[:, None, :]], axis=1)
    conv_out = lax.optimization_barrier(jnp.sum(window * conv_weight[None, :, :], axis=1)) + conv_bias
    u_mixer = jax.nn.silu(conv_out).astype(jnp.bfloat16)
    proj = jnp.dot(u_mixer, x_weight, preferred_element_type=jnp.float32)
    dt_low = proj[:, :RANK].astype(jnp.bfloat16)
    b_in = proj[:, RANK:RANK + NSTATE]
    c_out = proj[:, RANK + NSTATE:]
    step_size = jax.nn.softplus(jnp.dot(dt_low, dt_weight, preferred_element_type=jnp.float32) + dt_bias)
    rates = -jnp.exp(a_log)
    u_float = u_mixer.astype(jnp.float32)
    decay = jnp.exp(step_size[:, None, :] * rates[None, :, :])
    state = decay * ssm_state.astype(jnp.float32) + (step_size * u_float)[:, None, :] * b_in[:, :, None]
    y_mixer = lax.optimization_barrier(jnp.sum(state * c_out[:, :, None], axis=1)) + d_skip * u_float
    y_mixer = (y_mixer * jax.nn.silu(gate_z)).astype(jnp.bfloat16)
    hidden = residual.astype(jnp.float32) + jnp.dot(y_mixer, out_weight, preferred_element_type=jnp.float32)
    scale = lax.rsqrt(lax.optimization_barrier(jnp.mean(hidden * hidden, axis=-1, keepdims=True)) + 1e-06)
    normed = (hidden * scale * norm_gain).astype(jnp.bfloat16)
    moe = jnp.zeros(hidden.shape, jnp.float32)
    for expert in range(FLIGHT):
        lower = expert * HIDDEN_SIZE
        gate = jnp.dot(normed, w_gate[:, lower:lower + HIDDEN_SIZE], preferred_element_type=jnp.float32)
        upper = jnp.dot(normed, w_up[:, lower:lower + HIDDEN_SIZE], preferred_element_type=jnp.float32)
        act = (jax.nn.silu(gate) * upper).astype(jnp.bfloat16)
        out_e = jnp.dot(act, w_down[lower:lower + HIDDEN_SIZE, :], preferred_element_type=jnp.float32)
        coef = lax.optimization_barrier(jnp.sum(jnp.where(expert_ids == expert, route_weight, jnp.float32(0.0)), axis=1))
        moe = moe + coef[:, None] * out_e
    result = (hidden + moe).astype(jnp.bfloat16)
    return (result, state.astype(jnp.bfloat16))
```

```python
import functools

import jax
import jax.numpy as jnp
from jax import lax
from jax.experimental import pallas as pl
from jax.experimental.pallas import tpu as pltpu
from jax.sharding import PartitionSpec as P

FLIGHT = 2
CAP = 4
PACK = 4
MESH = pl.DeviceIdType.MESH


def push(src, dst, send_sem, recv_sem, peer):
    return pltpu.make_async_remote_copy(
        src_ref=src,
        dst_ref=dst,
        send_sem=send_sem,
        recv_sem=recv_sem,
        device_id={"chan": peer},
        device_id_type=MESH,
    )


def proj_kernel(n, part_ref, out_ref, landed, full, send_a, recv_a, send_b, recv_b):
    me = lax.axis_index("chan")
    barrier = pltpu.get_barrier_semaphore()

    @pl.loop(1, n)
    def _(k):
        pl.semaphore_signal(barrier, inc=1, device_id={"chan": (me + k) % n}, device_id_type=MESH)

    pl.semaphore_wait(barrier, n - 1)

    def scatter(owner, sender, peer):
        return push(part_ref.at[owner], landed.at[sender], send_a.at[owner], recv_a.at[sender], peer)

    def gather(slot, peer, sem):
        return push(full.at[slot], full.at[slot], send_b.at[sem], recv_b.at[slot], peer)

    @pl.loop(1, n)
    def _(k):
        peer = (me + k) % n
        scatter(peer, me, peer).start()

    def add(k, total):
        peer = (me + n - k) % n
        scatter(peer, peer, peer).wait_recv()
        return total + landed[peer].astype(jnp.float32)

    total = lax.fori_loop(1, n, add, part_ref[me].astype(jnp.float32))
    full[me] = total.astype(jnp.bfloat16)

    @pl.loop(1, n)
    def _(k):
        peer = (me + k) % n
        gather(me, peer, peer).start()

    @pl.loop(1, n)
    def _(k):
        peer = (me + n - k) % n
        gather(peer, peer, peer).wait_recv()

    out_ref[...] = full[...]

    @pl.loop(1, n)
    def _(k):
        peer = (me + k) % n
        scatter(peer, me, peer).wait_send()
        gather(me, peer, peer).wait_send()


def sum_proj(part, n):
    rows, cols = part.shape[1:]
    vmem = pl.BlockSpec(memory_space=pltpu.VMEM)
    return pl.pallas_call(
        functools.partial(proj_kernel, n),
        out_shape=jax.ShapeDtypeStruct(part.shape, jnp.bfloat16),
        in_specs=[vmem],
        out_specs=vmem,
        scratch_shapes=[
            pltpu.VMEM((n, rows, cols), jnp.bfloat16),
            pltpu.VMEM((n, rows, cols), jnp.bfloat16),
        ]
        + [pltpu.SemaphoreType.DMA((n,))] * 4,
        compiler_params=pltpu.CompilerParams(
            collective_id=0, has_side_effects=True, vmem_limit_bytes=16 * 2**20
        ),
    )(part)


def moe_kernel(
    n,
    y_ref,
    out_weight,
    residual_ref,
    gain_ref,
    ids_ref,
    ids_t_ref,
    route_ref,
    w_gate,
    w_up,
    w_down,
    result_ref,
    v_out,
    v_gate,
    v_up,
    v_down,
    part,
    own,
    pair_in,
    summed,
    mixed_in,
    hidden_ref,
    picked_f,
    picked,
    rows_in,
    rows,
    act,
    back_f,
    back,
    back_in,
    back_sum,
    final_in,
    local_sem,
    pair_sem,
    mixed_send,
    mixed_recv,
    rows_send,
    rows_recv,
    forward_send,
    final_send,
    final_recv,
):
    chips = n // 2
    half = chips // FLIGHT
    me = lax.axis_index("chan")
    chip, core = me // 2, me % 2
    other = 1 - core
    partner = chip * 2 + other
    row_dev, width = residual_ref.shape
    piece = width // PACK
    block = CAP * PACK
    f32, bf16 = jnp.float32, jnp.bfloat16

    load_out = pltpu.make_async_copy(out_weight, v_out, local_sem.at[0])
    loads = [
        pltpu.make_async_copy(src, dst, local_sem.at[i + 1])
        for i, (src, dst) in enumerate([(w_gate, v_gate), (w_up, v_up), (w_down, v_down)])
    ]
    load_out.start()

    barrier = pltpu.get_barrier_semaphore()
    pl.semaphore_signal(barrier, inc=1, device_id={"chan": partner}, device_id_type=MESH)

    @pl.loop(1, chips)
    def _(k):
        peer = ((chip + k) % chips) * 2 + core
        pl.semaphore_signal(barrier, inc=1, device_id={"chan": peer}, device_id_type=MESH)

    load_out.wait()
    for load in loads:
        load.start()

    tile = 512
    y_other = y_ref[other]

    @pl.loop(0, width // tile)
    def _(t):
        cols = pl.ds(pl.multiple_of(t * tile, tile), tile)
        value = jnp.dot(y_other, v_out[:, cols], preferred_element_type=f32)
        part[:, :, cols] = value.reshape(chips, row_dev, tile).astype(bf16)

    pl.semaphore_wait(barrier, chips)
    pair = push(part, pair_in, pair_sem.at[0], pair_sem.at[1], partner)
    pair.start()
    y_own = y_ref[core]

    @pl.loop(0, width // tile)
    def _(t):
        cols = pl.ds(pl.multiple_of(t * tile, tile), tile)
        value = jnp.dot(y_own, v_out[:, cols], preferred_element_type=f32)
        own[:, :, cols] = value.reshape(chips, row_dev, tile)

    pair.wait_recv()

    def mixed_copy(owner, sender):
        return push(
            summed.at[owner], mixed_in.at[sender], mixed_send.at[owner], mixed_recv.at[sender],
            owner * 2 + core,
        )

    @pl.loop(1, chips)
    def _(k):
        owner = (chip + k) % chips
        summed[owner] = (own[owner] + pair_in[owner].astype(f32)).astype(bf16)
        mixed_copy(owner, chip).start()

    hidden_ref[...] = residual_ref[...].astype(f32) + own[chip] + pair_in[chip].astype(f32)

    @pl.loop(1, chips)
    def _(k):
        sender = (chip + chips - k) % chips
        push(
            summed.at[sender], mixed_in.at[sender], mixed_send.at[sender], mixed_recv.at[sender],
            sender * 2 + core,
        ).wait_recv()
        hidden_ref[...] += mixed_in[sender].astype(f32)

    hidden = hidden_ref[...]
    scale = lax.rsqrt(jnp.mean(hidden * hidden, axis=-1, keepdims=True) + 1e-06)
    normed = (hidden * scale * gain_ref[...]).astype(bf16).astype(f32)

    ids, ids_t, route = ids_ref[...], ids_t_ref[...], route_ref[...]
    earlier = lax.broadcasted_iota(jnp.int32, (row_dev, row_dev), 1) < lax.broadcasted_iota(
        jnp.int32, (row_dev, row_dev), 0
    )
    masks = []
    for e in range(FLIGHT):
        named = jnp.where((ids[:, 0:1] == e) | (ids[:, 1:2] == e), 1.0, 0.0)
        named_row = jnp.where((ids_t[0:1, :] == e) | (ids_t[1:2, :] == e), 1.0, 0.0)
        place = jnp.sum(jnp.where(earlier, named_row, 0.0), axis=1, keepdims=True)
        masks.append([jnp.where(place == float(r), named, 0.0) for r in range(CAP)])
        for r in range(CAP):
            row = jnp.sum(masks[e][r] * normed, axis=0, keepdims=True)
            for q in range(PACK):
                at = q * CAP + r
                picked_f[e, at : at + 1, :] = row[:, q * piece : (q + 1) * piece]
    picked[...] = picked_f[...].astype(bf16)

    def rows_copy(slot_core, sender, peer_chip, peer_core, expert, sem):
        slot = slot_core * chips + sender
        return push(
            picked.at[expert], rows_in.at[slot], rows_send.at[sem], rows_recv.at[slot],
            peer_chip * 2 + peer_core,
        )

    def forward(sender, slot_core):
        slot = slot_core * chips + sender
        return push(
            rows_in.at[slot], rows_in.at[slot], forward_send.at[sender], rows_recv.at[slot], partner
        )

    my_expert = chip // half

    @pl.loop(1, chips)
    def _(k):
        peer = (chip + k) % chips
        rows_copy(core, chip, peer, core, peer // half, peer).start()

    rows_copy(core, chip, chip, other, my_expert, chip).start()
    rows_in[core * chips + chip] = picked[my_expert]

    @pl.loop(1, chips)
    def _(k):
        sender = (chip + chips - k) % chips
        rows_copy(core, sender, chip, other, my_expert, sender).wait_recv()
        forward(sender, core).start()

    @pl.loop(0, chips)
    def _(k):
        sender = (chip + chips - k) % chips
        forward(sender, other).wait_recv()

    count = n * CAP
    from_row = lax.broadcasted_iota(jnp.int32, (count, n * block), 0)
    from_col = lax.broadcasted_iota(jnp.int32, (count, n * block), 1)
    to_row = lax.broadcasted_iota(jnp.int32, (n * block, count), 1)
    to_col = lax.broadcasted_iota(jnp.int32, (n * block, count), 0)

    def packed_at(row, q):
        return (row // CAP) * block + q * CAP + row % CAP

    flat = rows_in[...].reshape(n * block, piece)
    for q in range(PACK):
        pick = jnp.where(from_col == packed_at(from_row, q), 1.0, 0.0).astype(bf16)
        rows[:, q * piece : (q + 1) * piece] = jnp.dot(
            pick, flat, preferred_element_type=f32
        ).astype(bf16)

    loads[0].wait()
    loads[1].wait()
    units = v_gate.shape[1]
    span = 512 if units % 512 == 0 else units

    @pl.loop(0, units // span)
    def _(t):
        cols = pl.ds(pl.multiple_of(t * span, span), span)
        gate = jnp.dot(rows[...], v_gate[:, cols], preferred_element_type=f32)
        upper = jnp.dot(rows[...], v_up[:, cols], preferred_element_type=f32)
        act[:, cols] = (jax.nn.silu(gate) * upper).astype(bf16)

    loads[2].wait()
    for q in range(PACK):
        out = jnp.dot(
            act[...], v_down[:, q * piece : (q + 1) * piece], preferred_element_type=f32
        ).astype(bf16)
        pick = jnp.where(to_col == packed_at(to_row, q), 1.0, 0.0).astype(bf16)
        moved = jnp.dot(pick, out, preferred_element_type=f32)
        if q == 0:
            back_f[...] = moved
        else:
            back_f[...] += moved
    back[...] = back_f[...].reshape(2, chips, block, piece).astype(bf16)

    swap = push(back.at[other], back_in, pair_sem.at[2], pair_sem.at[3], partner)
    swap.start()
    swap.wait_recv()

    def final_copy(owner, sender, peer):
        return push(
            back_sum.at[owner], final_in.at[sender], final_send.at[owner], final_recv.at[sender],
            peer * 2 + core,
        )

    @pl.loop(1, chips)
    def _(k):
        owner = (chip + k) % chips
        back_sum[owner] = (back[core, owner].astype(f32) + back_in[owner].astype(f32)).astype(bf16)
        final_copy(owner, chip, owner).start()

    final_in[chip] = (back[core, chip].astype(f32) + back_in[chip].astype(f32)).astype(bf16)

    @pl.loop(1, chips)
    def _(k):
        sender = (chip + chips - k) % chips
        final_copy(sender, sender, sender).wait_recv()

    hidden = hidden_ref[...]
    for e in range(FLIGHT):
        coef = jnp.sum(jnp.where(ids == e, route, 0.0), axis=1, keepdims=True)
        total = jnp.sum(final_in[e * half : (e + 1) * half].astype(f32), axis=0)
        weights = [coef * masks[e][r] for r in range(CAP)]
        if e == 0:
            moe = [None] * PACK
        for q in range(PACK):
            for r in range(CAP):
                at = q * CAP + r
                term = weights[r] * total[at : at + 1, :]
                moe[q] = term if moe[q] is None else moe[q] + term
    for q in range(PACK):
        cols = slice(q * piece, (q + 1) * piece)
        result_ref[:, cols] = (hidden[:, cols] + moe[q]).astype(bf16)

    pair.wait_send()
    swap.wait_send()
    rows_copy(core, chip, chip, other, my_expert, chip).wait_send()

    @pl.loop(1, chips)
    def _(k):
        peer = (chip + k) % chips
        mixed_copy(peer, chip).wait_send()
        rows_copy(core, chip, peer, core, peer // half, peer).wait_send()
        forward(peer, core).wait_send()
        final_copy(peer, chip, peer).wait_send()


def mix_experts(y, out_weight, residual, gain, ids, route, w_gate, w_up, w_down, n):
    chips = n // 2
    row_dev, width = residual.shape
    piece, block = width // PACK, CAP * PACK
    vmem, hbm = pl.BlockSpec(memory_space=pltpu.VMEM), pl.BlockSpec(memory_space=pl.ANY)
    bf16, f32 = jnp.bfloat16, jnp.float32
    dma = pltpu.SemaphoreType.DMA
    return pl.pallas_call(
        functools.partial(moe_kernel, n),
        out_shape=jax.ShapeDtypeStruct((row_dev, width), bf16),
        in_specs=[vmem, hbm, vmem, vmem, vmem, vmem, vmem, hbm, hbm, hbm],
        out_specs=vmem,
        scratch_shapes=[
            pltpu.VMEM(out_weight.shape, bf16),
            pltpu.VMEM(w_gate.shape, bf16),
            pltpu.VMEM(w_up.shape, bf16),
            pltpu.VMEM(w_down.shape, bf16),
            pltpu.VMEM((chips, row_dev, width), bf16),
            pltpu.VMEM((chips, row_dev, width), f32),
            pltpu.VMEM((chips, row_dev, width), bf16),
            pltpu.VMEM((chips, row_dev, width), bf16),
            pltpu.VMEM((chips, row_dev, width), bf16),
            pltpu.VMEM((row_dev, width), f32),
            pltpu.VMEM((FLIGHT, block, piece), f32),
            pltpu.VMEM((FLIGHT, block, piece), bf16),
            pltpu.VMEM((n, block, piece), bf16),
            pltpu.VMEM((n * CAP, width), bf16),
            pltpu.VMEM((n * CAP, w_gate.shape[1]), bf16),
            pltpu.VMEM((n * block, piece), f32),
            pltpu.VMEM((2, chips, block, piece), bf16),
            pltpu.VMEM((chips, block, piece), bf16),
            pltpu.VMEM((chips, block, piece), bf16),
            pltpu.VMEM((chips, block, piece), bf16),
            dma((4,)),
            dma((4,)),
            dma((chips,)),
            dma((chips,)),
            dma((chips,)),
            dma((n,)),
            dma((chips,)),
            dma((chips,)),
            dma((chips,)),
        ],
        compiler_params=pltpu.CompilerParams(
            collective_id=1, has_side_effects=True, vmem_limit_bytes=60 * 2**20
        ),
    )(y, out_weight, residual, gain.reshape(1, width), ids, ids.T, route, w_gate, w_up, w_down)


def shards(
    xz,
    conv_state,
    conv_weight,
    conv_bias,
    ssm_state,
    x_weight,
    dt_weight,
    dt_bias,
    a_log,
    d_skip,
    out_weight,
    residual,
    norm_gain,
    expert_ids,
    route_weight,
    w_gate,
    w_up,
    w_down,
):
    devices = lax.axis_size("chan")
    row_dev = residual.shape[0]
    rank_cols = dt_weight.shape[0]
    nstate = a_log.shape[0]
    x_new = xz[:, 0, :].astype(jnp.float32)
    gate_z = xz[:, 1, :].astype(jnp.float32)
    window = jnp.concatenate([conv_state.astype(jnp.float32), x_new[:, None, :]], axis=1)
    conv_out = jnp.sum(window * conv_weight[None, :, :], axis=1) + conv_bias
    u_mixer = jax.nn.silu(conv_out).astype(jnp.bfloat16)
    part = jnp.dot(u_mixer, x_weight, preferred_element_type=jnp.float32).astype(jnp.bfloat16)
    proj = sum_proj(part.reshape(devices, row_dev, -1), devices).reshape(part.shape)
    proj = proj.astype(jnp.float32)
    dt_low = proj[:, :rank_cols].astype(jnp.bfloat16)
    b_in = proj[:, rank_cols : rank_cols + nstate]
    c_out = proj[:, rank_cols + nstate :]
    step_size = jax.nn.softplus(
        jnp.dot(dt_low, dt_weight, preferred_element_type=jnp.float32) + dt_bias
    )
    rates = -jnp.exp(a_log)
    u_float = u_mixer.astype(jnp.float32)
    decay = jnp.exp(step_size[:, None, :] * rates[None, :, :])
    state = (
        decay * ssm_state.astype(jnp.float32) + (step_size * u_float)[:, None, :] * b_in[:, :, None]
    )
    y_mixer = jnp.sum(state * c_out[:, :, None], axis=1) + d_skip * u_float
    y_mixer = (y_mixer * jax.nn.silu(gate_z)).astype(jnp.bfloat16)
    new_state = state.astype(jnp.bfloat16)
    y_halves = y_mixer.reshape(devices // 2, 2, row_dev, -1).transpose(1, 0, 2, 3)
    result = mix_experts(
        y_halves.reshape(2, devices // 2 * row_dev, -1),
        out_weight,
        residual,
        norm_gain,
        expert_ids,
        route_weight,
        w_gate,
        w_up,
        w_down,
        devices,
    )
    return (result, new_state)


def solution(mesh):
    in_specs = (
        P("groups", None, "chan"),
        P("groups", None, "chan"),
        P(None, "chan"),
        P("chan"),
        P("groups", None, "chan"),
        P("chan", None),
        P(None, "chan"),
        P("chan"),
        P(None, "chan"),
        P("chan"),
        P("chan", None),
        P(("groups", "chan"), None),
        P(),
        P(("groups", "chan"), None),
        P(("groups", "chan"), None),
        P(None, "chan"),
        P(None, "chan"),
        P("chan", None),
    )
    out_specs = (P(("groups", "chan"), None), P("groups", None, "chan"))
    return jax.shard_map(shards, mesh=mesh, in_specs=in_specs, out_specs=out_specs, check_vma=False)
```

```python
import functools

import jax
import jax.numpy as jnp
from jax import lax
from jax.experimental import pallas as pl
from jax.experimental.pallas import tpu as pltpu
from jax.sharding import PartitionSpec as P

FLIGHT = 2
CAP = 4
PACK = 4
CHUNKS = 4
MESH = pl.DeviceIdType.MESH


def push(src, dst, send_sem, recv_sem, peer):
    return pltpu.make_async_remote_copy(
        src_ref=src,
        dst_ref=dst,
        send_sem=send_sem,
        recv_sem=recv_sem,
        device_id={"chan": peer},
        device_id_type=MESH,
    )


def proj_kernel(n, part_ref, out_ref, landed, full, send_a, recv_a, send_b, recv_b):
    me = lax.axis_index("chan")
    barrier = pltpu.get_barrier_semaphore()

    @pl.loop(1, n)
    def _(k):
        pl.semaphore_signal(barrier, inc=1, device_id={"chan": (me + k) % n}, device_id_type=MESH)

    pl.semaphore_wait(barrier, n - 1)

    def scatter(owner, sender, peer):
        return push(part_ref.at[owner], landed.at[sender], send_a.at[owner], recv_a.at[sender], peer)

    def gather(slot, peer, sem):
        return push(full.at[slot], full.at[slot], send_b.at[sem], recv_b.at[slot], peer)

    @pl.loop(1, n)
    def _(k):
        peer = (me + k) % n
        scatter(peer, me, peer).start()

    def add(k, total):
        peer = (me + n - k) % n
        scatter(peer, peer, peer).wait_recv()
        return total + landed[peer].astype(jnp.float32)

    total = lax.fori_loop(1, n, add, part_ref[me].astype(jnp.float32))
    full[me] = total.astype(jnp.bfloat16)

    @pl.loop(1, n)
    def _(k):
        peer = (me + k) % n
        gather(me, peer, peer).start()

    @pl.loop(1, n)
    def _(k):
        peer = (me + n - k) % n
        gather(peer, peer, peer).wait_recv()

    out_ref[...] = full[...]

    @pl.loop(1, n)
    def _(k):
        peer = (me + k) % n
        scatter(peer, me, peer).wait_send()
        gather(me, peer, peer).wait_send()


def sum_proj(part, n):
    rows, cols = part.shape[1:]
    vmem = pl.BlockSpec(memory_space=pltpu.VMEM)
    return pl.pallas_call(
        functools.partial(proj_kernel, n),
        out_shape=jax.ShapeDtypeStruct(part.shape, jnp.bfloat16),
        in_specs=[vmem],
        out_specs=vmem,
        scratch_shapes=[
            pltpu.VMEM((n, rows, cols), jnp.bfloat16),
            pltpu.VMEM((n, rows, cols), jnp.bfloat16),
        ]
        + [pltpu.SemaphoreType.DMA((n,))] * 4,
        compiler_params=pltpu.CompilerParams(
            collective_id=0, has_side_effects=True, vmem_limit_bytes=16 * 2**20
        ),
    )(part)


def moe_kernel(
    n,
    y_ref,
    out_weight,
    residual_ref,
    gain_ref,
    ids_ref,
    route_ref,
    w_gate,
    w_up,
    w_down,
    result_ref,
    v_out,
    v_gate,
    v_up,
    v_down,
    part,
    own,
    pair_in,
    side_out,
    side_in,
    summed,
    mixed_in,
    hidden_ref,
    picked_f,
    picked,
    rows_in,
    rows,
    act,
    back_f,
    back,
    back_in,
    back_sum,
    final_in,
    local_sem,
    swap_sem,
    pair_send,
    pair_recv,
    side_send,
    side_recv,
    mixed_send,
    mixed_recv,
    rows_send,
    rows_recv,
    forward_send,
    final_send,
    final_recv,
):
    chips = n // 2
    half = chips // FLIGHT
    me = lax.axis_index("chan")
    chip, core = me // 2, me % 2
    other = 1 - core
    partner = chip * 2 + other
    row_dev, width = residual_ref.shape
    piece = width // PACK
    block = CAP * PACK
    f32, bf16 = jnp.float32, jnp.bfloat16

    load_out = pltpu.make_async_copy(out_weight, v_out, local_sem.at[0])
    loads = [
        pltpu.make_async_copy(src, dst, local_sem.at[i + 1])
        for i, (src, dst) in enumerate([(w_gate, v_gate), (w_up, v_up), (w_down, v_down)])
    ]
    load_out.start()

    barrier = pltpu.get_barrier_semaphore()
    pl.semaphore_signal(barrier, inc=1, device_id={"chan": partner}, device_id_type=MESH)

    @pl.loop(1, chips)
    def _(k):
        peer = ((chip + k) % chips) * 2 + core
        pl.semaphore_signal(barrier, inc=1, device_id={"chan": peer}, device_id_type=MESH)

    load_out.wait()
    for load in loads:
        load.start()

    lines = chips // 2
    line, side = chip // 2, chip % 2
    across = (line * 2 + 1 - side) * 2 + core
    chunks = part.shape[0]
    tile = width // chunks
    y_other = y_ref[other]

    def pair_copy(c):
        return push(part.at[c], pair_in.at[c], pair_send.at[c], pair_recv.at[c], partner)

    def side_copy(c):
        return push(side_out.at[c], side_in.at[c], side_send.at[c], side_recv.at[c], across)

    def mixed_copy(c, owner, sender, peer):
        return push(
            summed.at[c, owner], mixed_in.at[c, sender],
            mixed_send.at[c, owner], mixed_recv.at[c, sender],
            (peer * 2 + side) * 2 + core,
        )

    for c in range(chunks):
        value = jnp.dot(
            y_other, v_out[:, c * tile : (c + 1) * tile], preferred_element_type=f32
        )
        part[c] = value.reshape(lines, 2, row_dev, tile).astype(bf16)
        if c == 0:
            pl.semaphore_wait(barrier, chips)
        pair_copy(c).start()
    y_own = y_ref[core]
    for c in range(chunks):
        value = jnp.dot(y_own, v_out[:, c * tile : (c + 1) * tile], preferred_element_type=f32)
        own[c] = value.reshape(lines, 2, row_dev, tile)
        pair_copy(c).wait_recv()
        side_out[c] = (own[c, :, 1 - side] + pair_in[c, :, 1 - side].astype(f32)).astype(bf16)
        side_copy(c).start()
    for c in range(chunks):
        side_copy(c).wait_recv()

        @pl.loop(1, lines)
        def _(k):
            owner = (line + k) % lines
            summed[c, owner] = (
                own[c, owner, side]
                + pair_in[c, owner, side].astype(f32)
                + side_in[c, owner].astype(f32)
            ).astype(bf16)
            mixed_copy(c, owner, line, owner).start()

        cols = slice(c * tile, (c + 1) * tile)
        hidden_ref[:, cols] = (
            residual_ref[:, cols].astype(f32)
            + own[c, line, side]
            + pair_in[c, line, side].astype(f32)
            + side_in[c, line].astype(f32)
        )
    for c in range(chunks):

        @pl.loop(1, lines)
        def _(k):
            sender = (line + lines - k) % lines
            mixed_copy(c, sender, sender, sender).wait_recv()
            hidden_ref[:, c * tile : (c + 1) * tile] += mixed_in[c, sender].astype(f32)

    hidden = hidden_ref[...]
    scale = lax.rsqrt(jnp.mean(hidden * hidden, axis=-1, keepdims=True) + 1e-06)
    normed = (hidden * scale * gain_ref[...]).astype(bf16).astype(f32)

    ids, route = ids_ref[...], route_ref[...]
    at_row = lax.broadcasted_iota(jnp.int32, (row_dev, row_dev), 0)
    at_col = lax.broadcasted_iota(jnp.int32, (row_dev, row_dev), 1)

    def upright(values):
        return jnp.sum(jnp.where(at_row == at_col, values, 0.0), axis=1, keepdims=True)

    masks = []
    for e in range(FLIGHT):
        named_row = jnp.where((ids[0:1, :] == e) | (ids[1:2, :] == e), 1.0, 0.0)
        named = upright(named_row)
        place = jnp.sum(jnp.where(at_col < at_row, named_row, 0.0), axis=1, keepdims=True)
        masks.append([jnp.where(place == float(r), named, 0.0) for r in range(CAP)])
        for r in range(CAP):
            row = jnp.sum(masks[e][r] * normed, axis=0, keepdims=True)
            for q in range(PACK):
                at = q * CAP + r
                picked_f[e, at : at + 1, :] = row[:, q * piece : (q + 1) * piece]
    picked[...] = picked_f[...].astype(bf16)

    def rows_copy(slot_core, sender, peer_chip, peer_core, expert, sem):
        slot = slot_core * chips + sender
        return push(
            picked.at[expert], rows_in.at[slot], rows_send.at[sem], rows_recv.at[slot],
            peer_chip * 2 + peer_core,
        )

    def forward(sender, slot_core):
        slot = slot_core * chips + sender
        return push(
            rows_in.at[slot], rows_in.at[slot], forward_send.at[sender], rows_recv.at[slot], partner
        )

    my_expert = chip // half

    @pl.loop(1, chips)
    def _(k):
        peer = (chip + k) % chips
        rows_copy(core, chip, peer, core, peer // half, peer).start()

    rows_copy(core, chip, chip, other, my_expert, chip).start()
    rows_in[core * chips + chip] = picked[my_expert]

    @pl.loop(1, chips)
    def _(k):
        sender = (chip + chips - k) % chips
        rows_copy(core, sender, chip, other, my_expert, sender).wait_recv()
        forward(sender, core).start()

    @pl.loop(0, chips)
    def _(k):
        sender = (chip + chips - k) % chips
        forward(sender, other).wait_recv()

    count = n * CAP
    from_row = lax.broadcasted_iota(jnp.int32, (count, n * block), 0)
    from_col = lax.broadcasted_iota(jnp.int32, (count, n * block), 1)
    to_row = lax.broadcasted_iota(jnp.int32, (n * block, count), 1)
    to_col = lax.broadcasted_iota(jnp.int32, (n * block, count), 0)

    def packed_at(row, q):
        return (row // CAP) * block + q * CAP + row % CAP

    flat = rows_in[...].reshape(n * block, piece)
    for q in range(PACK):
        pick = jnp.where(from_col == packed_at(from_row, q), 1.0, 0.0).astype(bf16)
        rows[:, q * piece : (q + 1) * piece] = jnp.dot(
            pick, flat, preferred_element_type=f32
        ).astype(bf16)

    loads[0].wait()
    loads[1].wait()
    units = v_gate.shape[1]
    span = 512 if units % 512 == 0 else units

    @pl.loop(0, units // span)
    def _(t):
        cols = pl.ds(pl.multiple_of(t * span, span), span)
        gate = jnp.dot(rows[...], v_gate[:, cols], preferred_element_type=f32)
        upper = jnp.dot(rows[...], v_up[:, cols], preferred_element_type=f32)
        act[:, cols] = (jax.nn.silu(gate) * upper).astype(bf16)

    loads[2].wait()
    for q in range(PACK):
        out = jnp.dot(
            act[...], v_down[:, q * piece : (q + 1) * piece], preferred_element_type=f32
        ).astype(bf16)
        pick = jnp.where(to_col == packed_at(to_row, q), 1.0, 0.0).astype(bf16)
        moved = jnp.dot(pick, out, preferred_element_type=f32)
        if q == 0:
            back_f[...] = moved
        else:
            back_f[...] += moved
    back[...] = back_f[...].reshape(2, chips, block, piece).astype(bf16)

    swap = push(back.at[other], back_in, swap_sem.at[0], swap_sem.at[1], partner)
    swap.start()
    swap.wait_recv()

    def final_copy(owner, sender, peer):
        return push(
            back_sum.at[owner], final_in.at[sender], final_send.at[owner], final_recv.at[sender],
            peer * 2 + core,
        )

    @pl.loop(1, chips)
    def _(k):
        owner = (chip + k) % chips
        back_sum[owner] = (back[core, owner].astype(f32) + back_in[owner].astype(f32)).astype(bf16)
        final_copy(owner, chip, owner).start()

    final_in[chip] = (back[core, chip].astype(f32) + back_in[chip].astype(f32)).astype(bf16)

    @pl.loop(1, chips)
    def _(k):
        sender = (chip + chips - k) % chips
        final_copy(sender, sender, sender).wait_recv()

    hidden = hidden_ref[...]
    for e in range(FLIGHT):
        coef = upright(jnp.sum(jnp.where(ids == e, route, 0.0), axis=0, keepdims=True))
        total = jnp.sum(final_in[e * half : (e + 1) * half].astype(f32), axis=0)
        weights = [coef * masks[e][r] for r in range(CAP)]
        if e == 0:
            moe = [None] * PACK
        for q in range(PACK):
            for r in range(CAP):
                at = q * CAP + r
                term = weights[r] * total[at : at + 1, :]
                moe[q] = term if moe[q] is None else moe[q] + term
    for q in range(PACK):
        cols = slice(q * piece, (q + 1) * piece)
        result_ref[:, cols] = (hidden[:, cols] + moe[q]).astype(bf16)

    for c in range(chunks):
        pair_copy(c).wait_send()
        side_copy(c).wait_send()

        @pl.loop(1, lines)
        def _(k):
            owner = (line + k) % lines
            mixed_copy(c, owner, line, owner).wait_send()

    swap.wait_send()
    rows_copy(core, chip, chip, other, my_expert, chip).wait_send()

    @pl.loop(1, chips)
    def _(k):
        peer = (chip + k) % chips
        rows_copy(core, chip, peer, core, peer // half, peer).wait_send()
        forward(peer, core).wait_send()
        final_copy(peer, chip, peer).wait_send()


def mix_experts(y, out_weight, residual, gain, ids, route, w_gate, w_up, w_down, n):
    chips = n // 2
    row_dev, width = residual.shape
    piece, block = width // PACK, CAP * PACK
    lines, tile = chips // 2, width // CHUNKS
    vmem, hbm = pl.BlockSpec(memory_space=pltpu.VMEM), pl.BlockSpec(memory_space=pl.ANY)
    bf16, f32 = jnp.bfloat16, jnp.float32
    dma = pltpu.SemaphoreType.DMA
    return pl.pallas_call(
        functools.partial(moe_kernel, n),
        out_shape=jax.ShapeDtypeStruct((row_dev, width), bf16),
        in_specs=[vmem, hbm, vmem, vmem, vmem, vmem, hbm, hbm, hbm],
        out_specs=vmem,
        scratch_shapes=[
            pltpu.VMEM(out_weight.shape, bf16),
            pltpu.VMEM(w_gate.shape, bf16),
            pltpu.VMEM(w_up.shape, bf16),
            pltpu.VMEM(w_down.shape, bf16),
            pltpu.VMEM((CHUNKS, lines, 2, row_dev, tile), bf16),
            pltpu.VMEM((CHUNKS, lines, 2, row_dev, tile), f32),
            pltpu.VMEM((CHUNKS, lines, 2, row_dev, tile), bf16),
            pltpu.VMEM((CHUNKS, lines, row_dev, tile), bf16),
            pltpu.VMEM((CHUNKS, lines, row_dev, tile), bf16),
            pltpu.VMEM((CHUNKS, lines, row_dev, tile), bf16),
            pltpu.VMEM((CHUNKS, lines, row_dev, tile), bf16),
            pltpu.VMEM((row_dev, width), f32),
            pltpu.VMEM((FLIGHT, block, piece), f32),
            pltpu.VMEM((FLIGHT, block, piece), bf16),
            pltpu.VMEM((n, block, piece), bf16),
            pltpu.VMEM((n * CAP, width), bf16),
            pltpu.VMEM((n * CAP, w_gate.shape[1]), bf16),
            pltpu.VMEM((n * block, piece), f32),
            pltpu.VMEM((2, chips, block, piece), bf16),
            pltpu.VMEM((chips, block, piece), bf16),
            pltpu.VMEM((chips, block, piece), bf16),
            pltpu.VMEM((chips, block, piece), bf16),
            dma((4,)),
            dma((2,)),
            dma((CHUNKS,)),
            dma((CHUNKS,)),
            dma((CHUNKS,)),
            dma((CHUNKS,)),
            dma((CHUNKS, lines)),
            dma((CHUNKS, lines)),
            dma((chips,)),
            dma((n,)),
            dma((chips,)),
            dma((chips,)),
            dma((chips,)),
        ],
        compiler_params=pltpu.CompilerParams(
            collective_id=1, has_side_effects=True, vmem_limit_bytes=60 * 2**20
        ),
    )(y, out_weight, residual, gain.reshape(1, width), ids.T, route.T, w_gate, w_up, w_down)


def shards(
    xz,
    conv_state,
    conv_weight,
    conv_bias,
    ssm_state,
    x_weight,
    dt_weight,
    dt_bias,
    a_log,
    d_skip,
    out_weight,
    residual,
    norm_gain,
    expert_ids,
    route_weight,
    w_gate,
    w_up,
    w_down,
):
    devices = lax.axis_size("chan")
    row_dev = residual.shape[0]
    rank_cols = dt_weight.shape[0]
    nstate = a_log.shape[0]
    x_new = xz[:, 0, :].astype(jnp.float32)
    gate_z = xz[:, 1, :].astype(jnp.float32)
    window = jnp.concatenate([conv_state.astype(jnp.float32), x_new[:, None, :]], axis=1)
    conv_out = jnp.sum(window * conv_weight[None, :, :], axis=1) + conv_bias
    u_mixer = jax.nn.silu(conv_out).astype(jnp.bfloat16)
    part = jnp.dot(u_mixer, x_weight, preferred_element_type=jnp.float32).astype(jnp.bfloat16)
    proj = sum_proj(part.reshape(devices, row_dev, -1), devices).reshape(part.shape)
    proj = proj.astype(jnp.float32)
    dt_low = proj[:, :rank_cols].astype(jnp.bfloat16)
    b_in = proj[:, rank_cols : rank_cols + nstate]
    c_out = proj[:, rank_cols + nstate :]
    step_size = jax.nn.softplus(
        jnp.dot(dt_low, dt_weight, preferred_element_type=jnp.float32) + dt_bias
    )
    rates = -jnp.exp(a_log)
    u_float = u_mixer.astype(jnp.float32)
    decay = jnp.exp(step_size[:, None, :] * rates[None, :, :])
    state = (
        decay * ssm_state.astype(jnp.float32) + (step_size * u_float)[:, None, :] * b_in[:, :, None]
    )
    y_mixer = jnp.sum(state * c_out[:, :, None], axis=1) + d_skip * u_float
    y_mixer = (y_mixer * jax.nn.silu(gate_z)).astype(jnp.bfloat16)
    new_state = state.astype(jnp.bfloat16)
    y_halves = y_mixer.reshape(devices // 2, 2, row_dev, -1).transpose(1, 0, 2, 3)
    result = mix_experts(
        y_halves.reshape(2, devices // 2 * row_dev, -1),
        out_weight,
        residual,
        norm_gain,
        expert_ids,
        route_weight,
        w_gate,
        w_up,
        w_down,
        devices,
    )
    return (result, new_state)


def solution(mesh):
    in_specs = (
        P("groups", None, "chan"),
        P("groups", None, "chan"),
        P(None, "chan"),
        P("chan"),
        P("groups", None, "chan"),
        P("chan", None),
        P(None, "chan"),
        P("chan"),
        P(None, "chan"),
        P("chan"),
        P("chan", None),
        P(("groups", "chan"), None),
        P(),
        P(("groups", "chan"), None),
        P(("groups", "chan"), None),
        P(None, "chan"),
        P(None, "chan"),
        P("chan", None),
    )
    out_specs = (P(("groups", "chan"), None), P("groups", None, "chan"))
    return jax.shard_map(shards, mesh=mesh, in_specs=in_specs, out_specs=out_specs, check_vma=False)
```

```python
import functools

import jax
import jax.numpy as jnp
from jax import lax
from jax.experimental import pallas as pl
from jax.experimental.pallas import tpu as pltpu
from jax.sharding import PartitionSpec as P

FLIGHT = 2
CAP = 4
PACK = 4
CHUNKS = 4
MESH = pl.DeviceIdType.MESH


def push(src, dst, send_sem, recv_sem, peer):
    return pltpu.make_async_remote_copy(
        src_ref=src,
        dst_ref=dst,
        send_sem=send_sem,
        recv_sem=recv_sem,
        device_id={"chan": peer},
        device_id_type=MESH,
    )


def proj_kernel(
    chips, part_ref, out_ref, pair_in, summed, landed, full,
    pair_sem, send_a, recv_a, send_b, recv_b, send_c, recv_c,
):
    me = lax.axis_index("chan")
    chip, core = me // 2, me % 2
    other = 1 - core
    partner = chip * 2 + other
    barrier = pltpu.get_barrier_semaphore()
    pl.semaphore_signal(barrier, inc=1, device_id={"chan": partner}, device_id_type=MESH)

    @pl.loop(1, chips)
    def _(k):
        peer = ((chip + k) % chips) * 2 + core
        pl.semaphore_signal(barrier, inc=1, device_id={"chan": peer}, device_id_type=MESH)

    pl.semaphore_wait(barrier, chips)
    pair = push(part_ref.at[other], pair_in, pair_sem.at[0], pair_sem.at[1], partner)

    def scatter(owner, sender, peer):
        return push(
            summed.at[owner], landed.at[sender], send_a.at[owner], recv_a.at[sender],
            peer * 2 + core,
        )

    def gather(sender, peer):
        here = full.at[sender, core]
        return push(here, here, send_b.at[peer], recv_b.at[sender], peer * 2 + core)

    def forward(sender, side):
        here = full.at[sender, side]
        return push(here, here, send_c.at[sender], recv_c.at[sender], partner)

    pair.start()
    pair.wait_recv()

    @pl.loop(1, chips)
    def _(k):
        peer = (chip + k) % chips
        summed[peer] = (
            part_ref[core, peer].astype(jnp.float32) + pair_in[peer].astype(jnp.float32)
        ).astype(jnp.bfloat16)
        scatter(peer, chip, peer).start()

    def add(k, total):
        peer = (chip + chips - k) % chips
        scatter(peer, peer, peer).wait_recv()
        return total + landed[peer].astype(jnp.float32)

    total = lax.fori_loop(
        1,
        chips,
        add,
        part_ref[core, chip].astype(jnp.float32) + pair_in[chip].astype(jnp.float32),
    )
    full[chip, core] = total.astype(jnp.bfloat16)

    @pl.loop(1, chips)
    def _(k):
        gather(chip, (chip + k) % chips).start()

    forward(chip, core).start()

    @pl.loop(1, chips)
    def _(k):
        sender = (chip + chips - k) % chips
        gather(sender, sender).wait_recv()
        forward(sender, core).start()

    @pl.loop(0, chips)
    def _(k):
        sender = (chip + chips - k) % chips
        forward(sender, other).wait_recv()

    out_ref[...] = full[...]
    pair.wait_send()
    forward(chip, core).wait_send()

    @pl.loop(1, chips)
    def _(k):
        peer = (chip + k) % chips
        scatter(peer, chip, peer).wait_send()
        gather(chip, peer).wait_send()
        forward(peer, core).wait_send()


def sum_proj(part, chips):
    rows, cols = part.shape[2:]
    vmem = pl.BlockSpec(memory_space=pltpu.VMEM)
    dma = pltpu.SemaphoreType.DMA
    return pl.pallas_call(
        functools.partial(proj_kernel, chips),
        out_shape=jax.ShapeDtypeStruct((chips, 2, rows, cols), jnp.bfloat16),
        in_specs=[vmem],
        out_specs=vmem,
        scratch_shapes=[pltpu.VMEM((chips, rows, cols), jnp.bfloat16)] * 3
        + [pltpu.VMEM((chips, 2, rows, cols), jnp.bfloat16), dma((2,))]
        + [dma((chips,))] * 6,
        compiler_params=pltpu.CompilerParams(
            collective_id=0, has_side_effects=True, vmem_limit_bytes=16 * 2**20
        ),
    )(part)


def moe_kernel(
    n,
    y_ref,
    out_weight,
    residual_ref,
    gain_ref,
    ids_ref,
    route_ref,
    w_gate,
    w_up,
    w_down,
    result_ref,
    v_out,
    v_gate,
    v_up,
    v_down,
    part,
    own,
    pair_in,
    side_out,
    side_in,
    summed,
    mixed_in,
    hidden_ref,
    picked_f,
    picked,
    rows_in,
    rows,
    act,
    back_f,
    back,
    back_in,
    back_sum,
    final_in,
    local_sem,
    swap_sem,
    pair_send,
    pair_recv,
    side_send,
    side_recv,
    mixed_send,
    mixed_recv,
    rows_send,
    rows_recv,
    forward_send,
    final_send,
    final_recv,
):
    chips = n // 2
    half = chips // FLIGHT
    me = lax.axis_index("chan")
    chip, core = me // 2, me % 2
    other = 1 - core
    partner = chip * 2 + other
    row_dev, width = residual_ref.shape
    piece = width // PACK
    block = CAP * PACK
    f32, bf16 = jnp.float32, jnp.bfloat16

    load_out = pltpu.make_async_copy(out_weight, v_out, local_sem.at[0])
    loads = [
        pltpu.make_async_copy(src, dst, local_sem.at[i + 1])
        for i, (src, dst) in enumerate([(w_gate, v_gate), (w_up, v_up), (w_down, v_down)])
    ]
    load_out.start()

    barrier = pltpu.get_barrier_semaphore()
    pl.semaphore_signal(barrier, inc=1, device_id={"chan": partner}, device_id_type=MESH)

    @pl.loop(1, chips)
    def _(k):
        peer = ((chip + k) % chips) * 2 + core
        pl.semaphore_signal(barrier, inc=1, device_id={"chan": peer}, device_id_type=MESH)

    load_out.wait()
    for load in loads:
        load.start()

    lines = chips // 2
    line, side = chip // 2, chip % 2
    across = (line * 2 + 1 - side) * 2 + core
    chunks = part.shape[0]
    tile = width // chunks
    y_other = y_ref[other]

    def pair_copy(c):
        return push(part.at[c], pair_in.at[c], pair_send.at[c], pair_recv.at[c], partner)

    def side_copy(c):
        return push(side_out.at[c], side_in.at[c], side_send.at[c], side_recv.at[c], across)

    def mixed_copy(c, owner, sender, peer):
        return push(
            summed.at[c, owner], mixed_in.at[c, sender],
            mixed_send.at[c, owner], mixed_recv.at[c, sender],
            (peer * 2 + side) * 2 + core,
        )

    for c in range(chunks):
        value = jnp.dot(
            y_other, v_out[:, c * tile : (c + 1) * tile], preferred_element_type=f32
        )
        part[c] = value.reshape(lines, 2, row_dev, tile).astype(bf16)
        if c == 0:
            pl.semaphore_wait(barrier, chips)
        pair_copy(c).start()
    y_own = y_ref[core]
    for c in range(chunks):
        value = jnp.dot(y_own, v_out[:, c * tile : (c + 1) * tile], preferred_element_type=f32)
        own[c] = value.reshape(lines, 2, row_dev, tile)
        pair_copy(c).wait_recv()
        side_out[c] = (own[c, :, 1 - side] + pair_in[c, :, 1 - side].astype(f32)).astype(bf16)
        side_copy(c).start()
    for c in range(chunks):
        side_copy(c).wait_recv()

        @pl.loop(1, lines)
        def _(k):
            owner = (line + k) % lines
            summed[c, owner] = (
                own[c, owner, side]
                + pair_in[c, owner, side].astype(f32)
                + side_in[c, owner].astype(f32)
            ).astype(bf16)
            mixed_copy(c, owner, line, owner).start()

        cols = slice(c * tile, (c + 1) * tile)
        hidden_ref[:, cols] = (
            residual_ref[:, cols].astype(f32)
            + own[c, line, side]
            + pair_in[c, line, side].astype(f32)
            + side_in[c, line].astype(f32)
        )
    for c in range(chunks):

        @pl.loop(1, lines)
        def _(k):
            sender = (line + lines - k) % lines
            mixed_copy(c, sender, sender, sender).wait_recv()
            hidden_ref[:, c * tile : (c + 1) * tile] += mixed_in[c, sender].astype(f32)

    hidden = hidden_ref[...]
    scale = lax.rsqrt(jnp.mean(hidden * hidden, axis=-1, keepdims=True) + 1e-06)
    normed = (hidden * scale * gain_ref[...]).astype(bf16).astype(f32)

    ids, route = ids_ref[...], route_ref[...]
    at_row = lax.broadcasted_iota(jnp.int32, (row_dev, row_dev), 0)
    at_col = lax.broadcasted_iota(jnp.int32, (row_dev, row_dev), 1)

    def upright(values):
        return jnp.sum(jnp.where(at_row == at_col, values, 0.0), axis=1, keepdims=True)

    masks = []
    for e in range(FLIGHT):
        named_row = jnp.where((ids[0:1, :] == e) | (ids[1:2, :] == e), 1.0, 0.0)
        named = upright(named_row)
        place = jnp.sum(jnp.where(at_col < at_row, named_row, 0.0), axis=1, keepdims=True)
        masks.append([jnp.where(place == float(r), named, 0.0) for r in range(CAP)])
        for r in range(CAP):
            row = jnp.sum(masks[e][r] * normed, axis=0, keepdims=True)
            for q in range(PACK):
                at = q * CAP + r
                picked_f[e, at : at + 1, :] = row[:, q * piece : (q + 1) * piece]
    picked[...] = picked_f[...].astype(bf16)

    def rows_copy(slot_core, sender, peer_chip, peer_core, expert, sem):
        slot = slot_core * chips + sender
        return push(
            picked.at[expert], rows_in.at[slot], rows_send.at[sem], rows_recv.at[slot],
            peer_chip * 2 + peer_core,
        )

    def forward(sender, slot_core):
        slot = slot_core * chips + sender
        return push(
            rows_in.at[slot], rows_in.at[slot], forward_send.at[sender], rows_recv.at[slot], partner
        )

    my_expert = chip // half

    @pl.loop(1, chips)
    def _(k):
        peer = (chip + k) % chips
        rows_copy(core, chip, peer, core, peer // half, peer).start()

    rows_copy(core, chip, chip, other, my_expert, chip).start()
    rows_in[core * chips + chip] = picked[my_expert]

    @pl.loop(1, chips)
    def _(k):
        sender = (chip + chips - k) % chips
        rows_copy(core, sender, chip, other, my_expert, sender).wait_recv()
        forward(sender, core).start()

    @pl.loop(0, chips)
    def _(k):
        sender = (chip + chips - k) % chips
        forward(sender, other).wait_recv()

    count = n * CAP
    from_row = lax.broadcasted_iota(jnp.int32, (count, n * block), 0)
    from_col = lax.broadcasted_iota(jnp.int32, (count, n * block), 1)
    to_row = lax.broadcasted_iota(jnp.int32, (n * block, count), 1)
    to_col = lax.broadcasted_iota(jnp.int32, (n * block, count), 0)

    def packed_at(row, q):
        return (row // CAP) * block + q * CAP + row % CAP

    flat = rows_in[...].reshape(n * block, piece)
    for q in range(PACK):
        pick = jnp.where(from_col == packed_at(from_row, q), 1.0, 0.0).astype(bf16)
        rows[:, q * piece : (q + 1) * piece] = jnp.dot(
            pick, flat, preferred_element_type=f32
        ).astype(bf16)

    loads[0].wait()
    loads[1].wait()
    units = v_gate.shape[1]
    span = 512 if units % 512 == 0 else units

    @pl.loop(0, units // span)
    def _(t):
        cols = pl.ds(pl.multiple_of(t * span, span), span)
        gate = jnp.dot(rows[...], v_gate[:, cols], preferred_element_type=f32)
        upper = jnp.dot(rows[...], v_up[:, cols], preferred_element_type=f32)
        act[:, cols] = (jax.nn.silu(gate) * upper).astype(bf16)

    loads[2].wait()
    for q in range(PACK):
        out = jnp.dot(
            act[...], v_down[:, q * piece : (q + 1) * piece], preferred_element_type=f32
        ).astype(bf16)
        pick = jnp.where(to_col == packed_at(to_row, q), 1.0, 0.0).astype(bf16)
        moved = jnp.dot(pick, out, preferred_element_type=f32)
        if q == 0:
            back_f[...] = moved
        else:
            back_f[...] += moved
    back[...] = back_f[...].reshape(2, chips, block, piece).astype(bf16)

    swap = push(back.at[other], back_in, swap_sem.at[0], swap_sem.at[1], partner)
    swap.start()
    swap.wait_recv()

    def final_copy(owner, sender, peer):
        return push(
            back_sum.at[owner], final_in.at[sender], final_send.at[owner], final_recv.at[sender],
            peer * 2 + core,
        )

    @pl.loop(1, chips)
    def _(k):
        owner = (chip + k) % chips
        back_sum[owner] = (back[core, owner].astype(f32) + back_in[owner].astype(f32)).astype(bf16)
        final_copy(owner, chip, owner).start()

    final_in[chip] = (back[core, chip].astype(f32) + back_in[chip].astype(f32)).astype(bf16)

    @pl.loop(1, chips)
    def _(k):
        sender = (chip + chips - k) % chips
        final_copy(sender, sender, sender).wait_recv()

    hidden = hidden_ref[...]
    for e in range(FLIGHT):
        coef = upright(jnp.sum(jnp.where(ids == e, route, 0.0), axis=0, keepdims=True))
        total = jnp.sum(final_in[e * half : (e + 1) * half].astype(f32), axis=0)
        weights = [coef * masks[e][r] for r in range(CAP)]
        if e == 0:
            moe = [None] * PACK
        for q in range(PACK):
            for r in range(CAP):
                at = q * CAP + r
                term = weights[r] * total[at : at + 1, :]
                moe[q] = term if moe[q] is None else moe[q] + term
    for q in range(PACK):
        cols = slice(q * piece, (q + 1) * piece)
        result_ref[:, cols] = (hidden[:, cols] + moe[q]).astype(bf16)

    for c in range(chunks):
        pair_copy(c).wait_send()
        side_copy(c).wait_send()

        @pl.loop(1, lines)
        def _(k):
            owner = (line + k) % lines
            mixed_copy(c, owner, line, owner).wait_send()

    swap.wait_send()
    rows_copy(core, chip, chip, other, my_expert, chip).wait_send()

    @pl.loop(1, chips)
    def _(k):
        peer = (chip + k) % chips
        rows_copy(core, chip, peer, core, peer // half, peer).wait_send()
        forward(peer, core).wait_send()
        final_copy(peer, chip, peer).wait_send()


def mix_experts(y, out_weight, residual, gain, ids, route, w_gate, w_up, w_down, n):
    chips = n // 2
    row_dev, width = residual.shape
    piece, block = width // PACK, CAP * PACK
    lines, tile = chips // 2, width // CHUNKS
    vmem, hbm = pl.BlockSpec(memory_space=pltpu.VMEM), pl.BlockSpec(memory_space=pl.ANY)
    bf16, f32 = jnp.bfloat16, jnp.float32
    dma = pltpu.SemaphoreType.DMA
    return pl.pallas_call(
        functools.partial(moe_kernel, n),
        out_shape=jax.ShapeDtypeStruct((row_dev, width), bf16),
        in_specs=[vmem, hbm, vmem, vmem, vmem, vmem, hbm, hbm, hbm],
        out_specs=vmem,
        scratch_shapes=[
            pltpu.VMEM(out_weight.shape, bf16),
            pltpu.VMEM(w_gate.shape, bf16),
            pltpu.VMEM(w_up.shape, bf16),
            pltpu.VMEM(w_down.shape, bf16),
            pltpu.VMEM((CHUNKS, lines, 2, row_dev, tile), bf16),
            pltpu.VMEM((CHUNKS, lines, 2, row_dev, tile), f32),
            pltpu.VMEM((CHUNKS, lines, 2, row_dev, tile), bf16),
            pltpu.VMEM((CHUNKS, lines, row_dev, tile), bf16),
            pltpu.VMEM((CHUNKS, lines, row_dev, tile), bf16),
            pltpu.VMEM((CHUNKS, lines, row_dev, tile), bf16),
            pltpu.VMEM((CHUNKS, lines, row_dev, tile), bf16),
            pltpu.VMEM((row_dev, width), f32),
            pltpu.VMEM((FLIGHT, block, piece), f32),
            pltpu.VMEM((FLIGHT, block, piece), bf16),
            pltpu.VMEM((n, block, piece), bf16),
            pltpu.VMEM((n * CAP, width), bf16),
            pltpu.VMEM((n * CAP, w_gate.shape[1]), bf16),
            pltpu.VMEM((n * block, piece), f32),
            pltpu.VMEM((2, chips, block, piece), bf16),
            pltpu.VMEM((chips, block, piece), bf16),
            pltpu.VMEM((chips, block, piece), bf16),
            pltpu.VMEM((chips, block, piece), bf16),
            dma((4,)),
            dma((2,)),
            dma((CHUNKS,)),
            dma((CHUNKS,)),
            dma((CHUNKS,)),
            dma((CHUNKS,)),
            dma((CHUNKS, lines)),
            dma((CHUNKS, lines)),
            dma((chips,)),
            dma((n,)),
            dma((chips,)),
            dma((chips,)),
            dma((chips,)),
        ],
        compiler_params=pltpu.CompilerParams(
            collective_id=1, has_side_effects=True, vmem_limit_bytes=60 * 2**20
        ),
    )(y, out_weight, residual, gain.reshape(1, width), ids.T, route.T, w_gate, w_up, w_down)


def shards(
    xz,
    conv_state,
    conv_weight,
    conv_bias,
    ssm_state,
    x_weight,
    dt_weight,
    dt_bias,
    a_log,
    d_skip,
    out_weight,
    residual,
    norm_gain,
    expert_ids,
    route_weight,
    w_gate,
    w_up,
    w_down,
):
    devices = lax.axis_size("chan")
    row_dev = residual.shape[0]
    rank_cols = dt_weight.shape[0]
    nstate = a_log.shape[0]
    x_new = xz[:, 0, :].astype(jnp.float32)
    gate_z = xz[:, 1, :].astype(jnp.float32)
    window = jnp.concatenate([conv_state.astype(jnp.float32), x_new[:, None, :]], axis=1)
    conv_out = jnp.sum(window * conv_weight[None, :, :], axis=1) + conv_bias
    u_mixer = jax.nn.silu(conv_out).astype(jnp.bfloat16)
    part = jnp.dot(u_mixer, x_weight, preferred_element_type=jnp.float32).astype(jnp.bfloat16)
    halves = part.reshape(devices // 2, 2, row_dev, -1).transpose(1, 0, 2, 3)
    proj = sum_proj(halves, devices // 2).reshape(part.shape)
    proj = proj.astype(jnp.float32)
    dt_low = proj[:, :rank_cols].astype(jnp.bfloat16)
    b_in = proj[:, rank_cols : rank_cols + nstate]
    c_out = proj[:, rank_cols + nstate :]
    step_size = jax.nn.softplus(
        jnp.dot(dt_low, dt_weight, preferred_element_type=jnp.float32) + dt_bias
    )
    rates = -jnp.exp(a_log)
    u_float = u_mixer.astype(jnp.float32)
    decay = jnp.exp(step_size[:, None, :] * rates[None, :, :])
    state = (
        decay * ssm_state.astype(jnp.float32) + (step_size * u_float)[:, None, :] * b_in[:, :, None]
    )
    y_mixer = jnp.sum(state * c_out[:, :, None], axis=1) + d_skip * u_float
    y_mixer = (y_mixer * jax.nn.silu(gate_z)).astype(jnp.bfloat16)
    new_state = state.astype(jnp.bfloat16)
    y_halves = y_mixer.reshape(devices // 2, 2, row_dev, -1).transpose(1, 0, 2, 3)
    result = mix_experts(
        y_halves.reshape(2, devices // 2 * row_dev, -1),
        out_weight,
        residual,
        norm_gain,
        expert_ids,
        route_weight,
        w_gate,
        w_up,
        w_down,
        devices,
    )
    return (result, new_state)


def solution(mesh):
    in_specs = (
        P("groups", None, "chan"),
        P("groups", None, "chan"),
        P(None, "chan"),
        P("chan"),
        P("groups", None, "chan"),
        P("chan", None),
        P(None, "chan"),
        P("chan"),
        P(None, "chan"),
        P("chan"),
        P("chan", None),
        P(("groups", "chan"), None),
        P(),
        P(("groups", "chan"), None),
        P(("groups", "chan"), None),
        P(None, "chan"),
        P(None, "chan"),
        P("chan", None),
    )
    out_specs = (P(("groups", "chan"), None), P("groups", None, "chan"))
    return jax.shard_map(shards, mesh=mesh, in_specs=in_specs, out_specs=out_specs, check_vma=False)
```

```python
import functools

import jax
import jax.numpy as jnp
from jax import lax
from jax.experimental import pallas as pl
from jax.experimental.pallas import tpu as pltpu
from jax.sharding import PartitionSpec as P

FLIGHT = 2
CAP = 4
PACK = 4
CHUNKS = 4
MESH = pl.DeviceIdType.MESH


def push(src, dst, send_sem, recv_sem, peer):
    return pltpu.make_async_remote_copy(
        src_ref=src,
        dst_ref=dst,
        send_sem=send_sem,
        recv_sem=recv_sem,
        device_id={"chan": peer},
        device_id_type=MESH,
    )


def proj_kernel(
    chips, part_ref, out_ref, pair_in, summed, landed, full,
    pair_sem, send_a, recv_a, send_b, recv_b, send_c, recv_c,
):
    me = lax.axis_index("chan")
    chip, core = me // 2, me % 2
    other = 1 - core
    partner = chip * 2 + other
    barrier = pltpu.get_barrier_semaphore()
    pl.semaphore_signal(barrier, inc=1, device_id={"chan": partner}, device_id_type=MESH)

    @pl.loop(1, chips)
    def _(k):
        peer = ((chip + k) % chips) * 2 + core
        pl.semaphore_signal(barrier, inc=1, device_id={"chan": peer}, device_id_type=MESH)

    pl.semaphore_wait(barrier, chips)
    pair = push(part_ref.at[other], pair_in, pair_sem.at[0], pair_sem.at[1], partner)

    def scatter(owner, sender, peer):
        return push(
            summed.at[owner], landed.at[sender], send_a.at[owner], recv_a.at[sender],
            peer * 2 + core,
        )

    def gather(sender, peer):
        here = full.at[sender, core]
        return push(here, here, send_b.at[peer], recv_b.at[sender], peer * 2 + core)

    def forward(sender, side):
        here = full.at[sender, side]
        return push(here, here, send_c.at[sender], recv_c.at[sender], partner)

    pair.start()
    pair.wait_recv()

    @pl.loop(1, chips)
    def _(k):
        peer = (chip + k) % chips
        summed[peer] = (
            part_ref[core, peer].astype(jnp.float32) + pair_in[peer].astype(jnp.float32)
        ).astype(jnp.bfloat16)
        scatter(peer, chip, peer).start()

    def add(k, total):
        peer = (chip + chips - k) % chips
        scatter(peer, peer, peer).wait_recv()
        return total + landed[peer].astype(jnp.float32)

    total = lax.fori_loop(
        1,
        chips,
        add,
        part_ref[core, chip].astype(jnp.float32) + pair_in[chip].astype(jnp.float32),
    )
    full[chip, core] = total.astype(jnp.bfloat16)

    @pl.loop(1, chips)
    def _(k):
        gather(chip, (chip + k) % chips).start()

    forward(chip, core).start()

    @pl.loop(1, chips)
    def _(k):
        sender = (chip + chips - k) % chips
        gather(sender, sender).wait_recv()
        forward(sender, core).start()

    @pl.loop(0, chips)
    def _(k):
        sender = (chip + chips - k) % chips
        forward(sender, other).wait_recv()

    out_ref[...] = full[...]
    pair.wait_send()
    forward(chip, core).wait_send()

    @pl.loop(1, chips)
    def _(k):
        peer = (chip + k) % chips
        scatter(peer, chip, peer).wait_send()
        gather(chip, peer).wait_send()
        forward(peer, core).wait_send()


def sum_proj(part, chips):
    rows, cols = part.shape[2:]
    vmem = pl.BlockSpec(memory_space=pltpu.VMEM)
    dma = pltpu.SemaphoreType.DMA
    return pl.pallas_call(
        functools.partial(proj_kernel, chips),
        out_shape=jax.ShapeDtypeStruct((chips, 2, rows, cols), jnp.bfloat16),
        in_specs=[vmem],
        out_specs=vmem,
        scratch_shapes=[pltpu.VMEM((chips, rows, cols), jnp.bfloat16)] * 3
        + [pltpu.VMEM((chips, 2, rows, cols), jnp.bfloat16), dma((2,))]
        + [dma((chips,))] * 6,
        compiler_params=pltpu.CompilerParams(
            collective_id=0, has_side_effects=True, vmem_limit_bytes=16 * 2**20
        ),
    )(part)


def moe_kernel(
    n,
    y_ref,
    out_weight,
    residual_ref,
    gain_ref,
    ids_ref,
    route_ref,
    w_gate,
    w_up,
    w_down,
    result_ref,
    v_out,
    v_gate,
    v_up,
    v_down,
    part,
    own,
    pair_in,
    side_out,
    side_in,
    summed,
    mixed_in,
    hidden_ref,
    picked_f,
    picked,
    rows_in,
    rows,
    act,
    back_f,
    back,
    back_in,
    back_sum,
    final_in,
    local_sem,
    swap_sem,
    pair_send,
    pair_recv,
    side_send,
    side_recv,
    mixed_send,
    mixed_recv,
    rows_send,
    rows_recv,
    forward_send,
    final_send,
    final_recv,
):
    chips = n // 2
    half = chips // FLIGHT
    me = lax.axis_index("chan")
    chip, core = me // 2, me % 2
    other = 1 - core
    partner = chip * 2 + other
    row_dev, width = residual_ref.shape
    piece = width // PACK
    block = CAP * PACK
    f32, bf16 = jnp.float32, jnp.bfloat16

    load_out = pltpu.make_async_copy(out_weight, v_out, local_sem.at[0])
    loads = [
        pltpu.make_async_copy(src, dst, local_sem.at[i + 1])
        for i, (src, dst) in enumerate([(w_gate, v_gate), (w_up, v_up), (w_down, v_down)])
    ]
    load_out.start()

    barrier = pltpu.get_barrier_semaphore()
    pl.semaphore_signal(barrier, inc=1, device_id={"chan": partner}, device_id_type=MESH)

    @pl.loop(1, chips)
    def _(k):
        peer = ((chip + k) % chips) * 2 + core
        pl.semaphore_signal(barrier, inc=1, device_id={"chan": peer}, device_id_type=MESH)

    load_out.wait()
    for load in loads:
        load.start()

    lines = chips // 2
    line, side = chip // 2, chip % 2
    across = (line * 2 + 1 - side) * 2 + core
    chunks = part.shape[0]
    tile = width // chunks
    y_other = y_ref[other]

    def pair_copy(c):
        return push(part.at[c], pair_in.at[c], pair_send.at[c], pair_recv.at[c], partner)

    def side_copy(c):
        return push(side_out.at[c], side_in.at[c], side_send.at[c], side_recv.at[c], across)

    def mixed_copy(c, owner, sender, peer):
        return push(
            summed.at[c, owner], mixed_in.at[c, sender],
            mixed_send.at[c, owner], mixed_recv.at[c, sender],
            (peer * 2 + side) * 2 + core,
        )

    for c in range(chunks):
        value = jnp.dot(
            y_other, v_out[:, c * tile : (c + 1) * tile], preferred_element_type=f32
        )
        part[c] = value.reshape(lines, 2, row_dev, tile).astype(bf16)
        if c == 0:
            pl.semaphore_wait(barrier, chips)
        pair_copy(c).start()
    y_own = y_ref[core]
    for c in range(chunks):
        value = jnp.dot(y_own, v_out[:, c * tile : (c + 1) * tile], preferred_element_type=f32)
        own[c] = value.reshape(lines, 2, row_dev, tile)
        pair_copy(c).wait_recv()
        side_out[c] = (own[c, :, 1 - side] + pair_in[c, :, 1 - side].astype(f32)).astype(bf16)
        side_copy(c).start()
    for c in range(chunks):
        side_copy(c).wait_recv()

        @pl.loop(1, lines)
        def _(k):
            owner = (line + k) % lines
            summed[c, owner] = (
                own[c, owner, side]
                + pair_in[c, owner, side].astype(f32)
                + side_in[c, owner].astype(f32)
            ).astype(bf16)
            mixed_copy(c, owner, line, owner).start()

        cols = slice(c * tile, (c + 1) * tile)
        hidden_ref[:, cols] = (
            residual_ref[:, cols].astype(f32)
            + own[c, line, side]
            + pair_in[c, line, side].astype(f32)
            + side_in[c, line].astype(f32)
        )
    for c in range(chunks):

        @pl.loop(1, lines)
        def _(k):
            sender = (line + lines - k) % lines
            mixed_copy(c, sender, sender, sender).wait_recv()
            hidden_ref[:, c * tile : (c + 1) * tile] += mixed_in[c, sender].astype(f32)

    hidden = hidden_ref[...]
    scale = lax.rsqrt(jnp.mean(hidden * hidden, axis=-1, keepdims=True) + 1e-06)
    normed = (hidden * scale * gain_ref[...]).astype(bf16).astype(f32)

    ids, route = ids_ref[...], route_ref[...]
    at_row = lax.broadcasted_iota(jnp.int32, (row_dev, row_dev), 0)
    at_col = lax.broadcasted_iota(jnp.int32, (row_dev, row_dev), 1)

    def upright(values):
        return jnp.sum(jnp.where(at_row == at_col, values, 0.0), axis=1, keepdims=True)

    masks = []
    for e in range(FLIGHT):
        named_row = jnp.where((ids[0:1, :] == e) | (ids[1:2, :] == e), 1.0, 0.0)
        named = upright(named_row)
        place = jnp.sum(jnp.where(at_col < at_row, named_row, 0.0), axis=1, keepdims=True)
        masks.append([jnp.where(place == float(r), named, 0.0) for r in range(CAP)])
        for r in range(CAP):
            row = jnp.sum(masks[e][r] * normed, axis=0, keepdims=True)
            for q in range(PACK):
                at = q * CAP + r
                picked_f[e, at : at + 1, :] = row[:, q * piece : (q + 1) * piece]
    picked[...] = picked_f[...].astype(bf16)

    def rows_copy(slot_core, sender, peer_chip, peer_core, expert, sem):
        slot = slot_core * chips + sender
        return push(
            picked.at[expert], rows_in.at[slot], rows_send.at[sem], rows_recv.at[slot],
            peer_chip * 2 + peer_core,
        )

    def forward(sender, slot_core):
        slot = slot_core * chips + sender
        return push(
            rows_in.at[slot], rows_in.at[slot], forward_send.at[sender], rows_recv.at[slot], partner
        )

    my_expert = chip // half

    @pl.loop(1, chips)
    def _(k):
        peer = (chip + k) % chips
        rows_copy(core, chip, peer, core, peer // half, peer).start()

    rows_copy(core, chip, chip, other, my_expert, chip).start()
    rows_in[core * chips + chip] = picked[my_expert]

    @pl.loop(1, chips)
    def _(k):
        sender = (chip + chips - k) % chips
        rows_copy(core, sender, chip, other, my_expert, sender).wait_recv()
        forward(sender, core).start()

    @pl.loop(0, chips)
    def _(k):
        sender = (chip + chips - k) % chips
        forward(sender, other).wait_recv()

    count = n * CAP
    from_row = lax.broadcasted_iota(jnp.int32, (count, n * block), 0)
    from_col = lax.broadcasted_iota(jnp.int32, (count, n * block), 1)
    to_row = lax.broadcasted_iota(jnp.int32, (n * block, count), 1)
    to_col = lax.broadcasted_iota(jnp.int32, (n * block, count), 0)

    def packed_at(row, q):
        return (row // CAP) * block + q * CAP + row % CAP

    flat = rows_in[...].reshape(n * block, piece)
    for q in range(PACK):
        pick = jnp.where(from_col == packed_at(from_row, q), 1.0, 0.0).astype(bf16)
        rows[:, q * piece : (q + 1) * piece] = jnp.dot(
            pick, flat, preferred_element_type=f32
        ).astype(bf16)

    loads[0].wait()
    loads[1].wait()
    units = v_gate.shape[1]
    span = 512 if units % 512 == 0 else units

    for t in range(units // span):
        cols = slice(t * span, (t + 1) * span)
        gate = jnp.dot(rows[...], v_gate[:, cols], preferred_element_type=f32)
        upper = jnp.dot(rows[...], v_up[:, cols], preferred_element_type=f32)
        act[:, cols] = (jax.nn.silu(gate) * upper).astype(bf16)

    loads[2].wait()
    for q in range(PACK):
        out = jnp.dot(
            act[...], v_down[:, q * piece : (q + 1) * piece], preferred_element_type=f32
        ).astype(bf16)
        pick = jnp.where(to_col == packed_at(to_row, q), 1.0, 0.0).astype(bf16)
        moved = jnp.dot(pick, out, preferred_element_type=f32)
        if q == 0:
            back_f[...] = moved
        else:
            back_f[...] += moved
    back[...] = back_f[...].reshape(2, chips, block, piece).astype(bf16)

    swap = push(back.at[other], back_in, swap_sem.at[0], swap_sem.at[1], partner)
    swap.start()
    swap.wait_recv()

    def final_copy(owner, sender, peer):
        return push(
            back_sum.at[owner], final_in.at[sender], final_send.at[owner], final_recv.at[sender],
            peer * 2 + core,
        )

    @pl.loop(1, chips)
    def _(k):
        owner = (chip + k) % chips
        back_sum[owner] = (back[core, owner].astype(f32) + back_in[owner].astype(f32)).astype(bf16)
        final_copy(owner, chip, owner).start()

    final_in[chip] = (back[core, chip].astype(f32) + back_in[chip].astype(f32)).astype(bf16)

    @pl.loop(1, chips)
    def _(k):
        sender = (chip + chips - k) % chips
        final_copy(sender, sender, sender).wait_recv()

    hidden = hidden_ref[...]
    for e in range(FLIGHT):
        coef = upright(jnp.sum(jnp.where(ids == e, route, 0.0), axis=0, keepdims=True))
        total = jnp.sum(final_in[e * half : (e + 1) * half].astype(f32), axis=0)
        weights = [coef * masks[e][r] for r in range(CAP)]
        if e == 0:
            moe = [None] * PACK
        for q in range(PACK):
            for r in range(CAP):
                at = q * CAP + r
                term = weights[r] * total[at : at + 1, :]
                moe[q] = term if moe[q] is None else moe[q] + term
    for q in range(PACK):
        cols = slice(q * piece, (q + 1) * piece)
        result_ref[:, cols] = (hidden[:, cols] + moe[q]).astype(bf16)

    for c in range(chunks):
        pair_copy(c).wait_send()
        side_copy(c).wait_send()

        @pl.loop(1, lines)
        def _(k):
            owner = (line + k) % lines
            mixed_copy(c, owner, line, owner).wait_send()

    swap.wait_send()
    rows_copy(core, chip, chip, other, my_expert, chip).wait_send()

    @pl.loop(1, chips)
    def _(k):
        peer = (chip + k) % chips
        rows_copy(core, chip, peer, core, peer // half, peer).wait_send()
        forward(peer, core).wait_send()
        final_copy(peer, chip, peer).wait_send()


def mix_experts(y, out_weight, residual, gain, ids, route, w_gate, w_up, w_down, n):
    chips = n // 2
    row_dev, width = residual.shape
    piece, block = width // PACK, CAP * PACK
    lines, tile = chips // 2, width // CHUNKS
    vmem, hbm = pl.BlockSpec(memory_space=pltpu.VMEM), pl.BlockSpec(memory_space=pl.ANY)
    bf16, f32 = jnp.bfloat16, jnp.float32
    dma = pltpu.SemaphoreType.DMA
    return pl.pallas_call(
        functools.partial(moe_kernel, n),
        out_shape=jax.ShapeDtypeStruct((row_dev, width), bf16),
        in_specs=[vmem, hbm, vmem, vmem, vmem, vmem, hbm, hbm, hbm],
        out_specs=vmem,
        scratch_shapes=[
            pltpu.VMEM(out_weight.shape, bf16),
            pltpu.VMEM(w_gate.shape, bf16),
            pltpu.VMEM(w_up.shape, bf16),
            pltpu.VMEM(w_down.shape, bf16),
            pltpu.VMEM((CHUNKS, lines, 2, row_dev, tile), bf16),
            pltpu.VMEM((CHUNKS, lines, 2, row_dev, tile), f32),
            pltpu.VMEM((CHUNKS, lines, 2, row_dev, tile), bf16),
            pltpu.VMEM((CHUNKS, lines, row_dev, tile), bf16),
            pltpu.VMEM((CHUNKS, lines, row_dev, tile), bf16),
            pltpu.VMEM((CHUNKS, lines, row_dev, tile), bf16),
            pltpu.VMEM((CHUNKS, lines, row_dev, tile), bf16),
            pltpu.VMEM((row_dev, width), f32),
            pltpu.VMEM((FLIGHT, block, piece), f32),
            pltpu.VMEM((FLIGHT, block, piece), bf16),
            pltpu.VMEM((n, block, piece), bf16),
            pltpu.VMEM((n * CAP, width), bf16),
            pltpu.VMEM((n * CAP, w_gate.shape[1]), bf16),
            pltpu.VMEM((n * block, piece), f32),
            pltpu.VMEM((2, chips, block, piece), bf16),
            pltpu.VMEM((chips, block, piece), bf16),
            pltpu.VMEM((chips, block, piece), bf16),
            pltpu.VMEM((chips, block, piece), bf16),
            dma((4,)),
            dma((2,)),
            dma((CHUNKS,)),
            dma((CHUNKS,)),
            dma((CHUNKS,)),
            dma((CHUNKS,)),
            dma((CHUNKS, lines)),
            dma((CHUNKS, lines)),
            dma((chips,)),
            dma((n,)),
            dma((chips,)),
            dma((chips,)),
            dma((chips,)),
        ],
        compiler_params=pltpu.CompilerParams(
            collective_id=1, has_side_effects=True, vmem_limit_bytes=60 * 2**20
        ),
    )(y, out_weight, residual, gain.reshape(1, width), ids.T, route.T, w_gate, w_up, w_down)


def shards(
    xz,
    conv_state,
    conv_weight,
    conv_bias,
    ssm_state,
    x_weight,
    dt_weight,
    dt_bias,
    a_log,
    d_skip,
    out_weight,
    residual,
    norm_gain,
    expert_ids,
    route_weight,
    w_gate,
    w_up,
    w_down,
):
    devices = lax.axis_size("chan")
    row_dev = residual.shape[0]
    rank_cols = dt_weight.shape[0]
    nstate = a_log.shape[0]
    x_new = xz[:, 0, :].astype(jnp.float32)
    gate_z = xz[:, 1, :].astype(jnp.float32)
    window = jnp.concatenate([conv_state.astype(jnp.float32), x_new[:, None, :]], axis=1)
    conv_out = jnp.sum(window * conv_weight[None, :, :], axis=1) + conv_bias
    u_mixer = jax.nn.silu(conv_out).astype(jnp.bfloat16)
    part = jnp.dot(u_mixer, x_weight, preferred_element_type=jnp.float32).astype(jnp.bfloat16)
    halves = part.reshape(devices // 2, 2, row_dev, -1).transpose(1, 0, 2, 3)
    proj = sum_proj(halves, devices // 2).reshape(part.shape)
    proj = proj.astype(jnp.float32)
    dt_low = proj[:, :rank_cols].astype(jnp.bfloat16)
    b_in = proj[:, rank_cols : rank_cols + nstate]
    c_out = proj[:, rank_cols + nstate :]
    step_size = jax.nn.softplus(
        jnp.dot(dt_low, dt_weight, preferred_element_type=jnp.float32) + dt_bias
    )
    rates = -jnp.exp(a_log)
    u_float = u_mixer.astype(jnp.float32)
    decay = jnp.exp(step_size[:, None, :] * rates[None, :, :])
    state = (
        decay * ssm_state.astype(jnp.float32) + (step_size * u_float)[:, None, :] * b_in[:, :, None]
    )
    y_mixer = jnp.sum(state * c_out[:, :, None], axis=1) + d_skip * u_float
    y_mixer = (y_mixer * jax.nn.silu(gate_z)).astype(jnp.bfloat16)
    new_state = state.astype(jnp.bfloat16)
    y_halves = y_mixer.reshape(devices // 2, 2, row_dev, -1).transpose(1, 0, 2, 3)
    result = mix_experts(
        y_halves.reshape(2, devices // 2 * row_dev, -1),
        out_weight,
        residual,
        norm_gain,
        expert_ids,
        route_weight,
        w_gate,
        w_up,
        w_down,
        devices,
    )
    return (result, new_state)


def solution(mesh):
    in_specs = (
        P("groups", None, "chan"),
        P("groups", None, "chan"),
        P(None, "chan"),
        P("chan"),
        P("groups", None, "chan"),
        P("chan", None),
        P(None, "chan"),
        P("chan"),
        P(None, "chan"),
        P("chan"),
        P("chan", None),
        P(("groups", "chan"), None),
        P(),
        P(("groups", "chan"), None),
        P(("groups", "chan"), None),
        P(None, "chan"),
        P(None, "chan"),
        P("chan", None),
    )
    out_specs = (P(("groups", "chan"), None), P("groups", None, "chan"))
    return jax.shard_map(shards, mesh=mesh, in_specs=in_specs, out_specs=out_specs, check_vma=False)
```
